32 devices in a mesh: section: 16 (over z, y, x), expert: 2 (over core).
Axes of the slice: x: 2, y: 2, z: 4, core: 2. Of those that a mesh axis runs over, the one named last changes fastest.
Arguments:
- state: bfloat16 [16, 2048, 3584], P('section', 'expert'), may hold values from -6 to 6
- norm_gain: float32 [16, 3584], P('section'), may hold values from 0.1 to 1.9
- router: bfloat16 [16, 3584, 128], P('section'), may hold values from -0.1875 to 0.1875
- w_gate: bfloat16 [16, 3584, 1024], P('section', None, 'expert'), may hold values from -0.09375 to 0.09375
- w_up: bfloat16 [16, 3584, 1024], P('section', None, 'expert'), may hold values from -0.09375 to 0.09375
- w_down: bfloat16 [16, 1024, 3584], P('section', 'expert'), may hold values from -0.25 to 0.25
- route_ids: int32 [1, 16, 2048, 8], P(None, 'section', 'expert'), may hold values from 0 to 127, as said below
Outputs:
- state_out: bfloat16 [16, 2048, 3584], P('section', 'expert')
The draws below stay inside these ranges and needn't reach their ends.
Inputs may be any that keep to these rules, and one draw needn't show every extreme that they name: `route_ids`: each row names 8 different experts; expert 0 is the expert whose weights are given.
All inputs are finite; a program needn't handle non-finite values.
Results may differ from the reference program's by a relative error of at most 0.002.
Values may be sent and summed in bfloat16 or wider, within the bound.
A program may use at most 128 MiB of HBM per device.

```python
import jax
import jax.numpy as jnp
from jax import lax

D = 3584
HE_DEV = 512
EXPERTS = 128
TOP = 8
TICKS = 1
TOK_DEV = 1024
CAP = 128
EXPERT_HID = 1024
MB_TOK = 2048
LAYERS = 16
N_EXPERT = 2


def draw_route_ids(key, part):
    keys = jax.random.split(key, 5)
    rows_shape = (TICKS, LAYERS, MB_TOK)
    level = jax.random.randint(keys[0], (TICKS, LAYERS, MB_TOK // TOK_DEV), 1, 5)
    level_rows = jnp.repeat(level, TOK_DEV, axis=2)
    coin = jax.random.randint(keys[1], rows_shape, 0, 16)
    chosen = coin < level_rows
    base = jax.random.randint(keys[2], rows_shape, 0, EXPERTS - 1)
    stride = jax.random.randint(keys[3], rows_shape, 1, (EXPERTS - 2) // 7 + 1)
    position = jax.random.randint(keys[4], rows_shape, 0, TOP)
    order = jnp.arange(TOP).astype(jnp.int32)
    ids = 1 + (base[..., None] + order * stride[..., None]) % (EXPERTS - 1)
    ids = jnp.where(chosen[..., None] & (order == position[..., None]), 0, ids)
    return ids.astype(jnp.int32)


def block_scale(own_key, dims, cuts, low, top_value):
    level, own = 1.0, jax.random.fold_in(own_key, 6)
    for dim, parts in cuts:
        steps = jnp.exp(jax.random.uniform(jax.random.fold_in(own, dim), (parts,), jnp.float32, low / len(cuts), top_value / len(cuts)))
        level = level * jnp.repeat(steps, dims[dim] // parts).reshape([-1 if axis == dim else 1 for axis in range(len(dims))])
    return level


def noise(rng, dims, spread, reach, pieces=(), held_as=jnp.bfloat16):
    drawn = spread * jax.random.normal(rng, dims, jnp.float32)
    if pieces:
        drawn = drawn * block_scale(rng, dims, pieces, -0.22, 0.18)
    return jnp.clip(drawn, -reach, reach).astype(held_as)


def setup_inputs(seed: int = 0) -> dict:
    streams_of = jax.random.split(jax.random.key(seed), 8)
    state = noise(streams_of[0], (LAYERS, MB_TOK, D), 1.0, 6.0, ((0, 16), (1, 2)))
    norm_gain = jnp.clip(1.0 + 0.18 * jax.random.normal(streams_of[1], (LAYERS, D), jnp.float32), 0.1, 1.9)
    router = noise(streams_of[2], (LAYERS, D, EXPERTS), (D // 4) ** -0.5, 0.1875, ((0, 16),))
    w_gate = noise(streams_of[3], (LAYERS, D, EXPERT_HID), D ** -0.5, 0.09375, ((0, 16), (2, 2)))
    w_up = noise(streams_of[4], (LAYERS, D, EXPERT_HID), D ** -0.5, 0.09375, ((0, 16), (2, 2)))
    w_down = noise(streams_of[5], (LAYERS, EXPERT_HID, D), HE_DEV ** -0.5, 0.25, ((0, 16), (1, 2)))
    route_ids = draw_route_ids(jax.random.fold_in(streams_of[7], 71), 0)
    return dict(state=state, norm_gain=norm_gain, router=router, w_gate=w_gate, w_up=w_up, w_down=w_down, route_ids=route_ids)


def segment_step(args):
    h, gain, router, w_gate, w_up, w_down, ids = args
    h32 = h.astype(jnp.float32)
    var = lax.optimization_barrier(jnp.mean(h32 * h32, axis=-1, keepdims=True))
    normed = (h32 * lax.rsqrt(var + 1e-06) * gain).astype(jnp.bfloat16)
    scores = jax.nn.sigmoid(jnp.dot(normed, router, preferred_element_type=jnp.float32))
    expert_iota = jnp.arange(EXPERTS).astype(jnp.int32)
    picked = lax.optimization_barrier(jnp.sum((ids[:, :, None] == expert_iota[None, None, :]).astype(jnp.float32), axis=1))
    weight = 2.5 * scores[:, 0] * picked[:, 0] / lax.optimization_barrier(jnp.sum(scores * picked, axis=-1))
    chosen = lax.optimization_barrier(jnp.sum((ids == 0).astype(jnp.int32), axis=-1)).reshape(N_EXPERT, TOK_DEV)
    slot = jnp.cumsum(chosen, axis=-1).astype(jnp.int32) - chosen
    kept = (chosen > 0) & (slot < CAP)
    slot_iota = jnp.arange(CAP).astype(jnp.int32)
    onehot = (kept[:, None, :] & (slot[:, None, :] == slot_iota[None, :, None])).astype(jnp.float32)
    blocks = normed.astype(jnp.float32).reshape(N_EXPERT, TOK_DEV, D)
    packed = jnp.einsum('bjt,btd->bjd', onehot, blocks, precision=lax.Precision.HIGHEST)
    packed = packed.astype(jnp.bfloat16).reshape(N_EXPERT * CAP, D)
    gate = jnp.dot(packed, w_gate, preferred_element_type=jnp.float32)
    upper = jnp.dot(packed, w_up, preferred_element_type=jnp.float32)
    active = (jax.nn.silu(gate) * upper).astype(jnp.bfloat16)
    expert_out = jnp.zeros((N_EXPERT * CAP, D), jnp.float32)
    for block in range(N_EXPERT):
        part = jnp.dot(active[:, block * HE_DEV:(block + 1) * HE_DEV], w_down[block * HE_DEV:(block + 1) * HE_DEV], preferred_element_type=jnp.float32)
        part = lax.optimization_barrier(part.astype(jnp.bfloat16)).astype(jnp.float32)
        expert_out = expert_out + part
    share = jnp.einsum('bjt,bt->bj', onehot, weight.reshape(N_EXPERT, TOK_DEV), precision=lax.Precision.HIGHEST)
    scaled = expert_out.reshape(N_EXPERT, CAP, D) * share[:, :, None]
    delta = jnp.einsum('bjt,bjd->btd', onehot, scaled, precision=lax.Precision.HIGHEST).reshape(N_EXPERT * TOK_DEV, D)
    return (h32 + delta).astype(jnp.bfloat16)

def reference(state, norm_gain, router, w_gate, w_up, w_down, route_ids):
    current = state
    for tick in range(TICKS):
        current = lax.map(segment_step, (current, norm_gain, router, w_gate, w_up, w_down, route_ids[tick]))
        current = jnp.roll(current, 1, axis=0)
    return current
```

```python
import functools

import jax
import jax.numpy as jnp
from jax import lax
from jax.experimental import pallas as pl
from jax.experimental.pallas import tpu as pltpu
from jax.sharding import PartitionSpec as P

VMEM_LIMIT = 56 * 1024 * 1024
CHUNKS = (1, 1, 2, 3)
NOWHERE = -(1 << 20)


def passed_along(x, axis, by):
    devices = lax.axis_size(axis)
    return lax.ppermute(x, axis, [(i, (i + by) % devices) for i in range(devices)])


def after(x, done):
    return lax.optimization_barrier((x, done))[0]


def onehot_to(pos, base, size):
    places = lax.broadcasted_iota(jnp.int32, (size, pos.shape[1]), 0) + base
    return jnp.where(places == pos, 1.0, 0.0).astype(jnp.bfloat16)


def pack_kernel(first, pos_a, pos_b, rows_a, rows_b, out):
    size = out.shape[0]
    base = (pl.program_id(0) + first) * size
    total = jnp.dot(onehot_to(pos_a[...], base, size), rows_a[...], preferred_element_type=jnp.float32)
    total += jnp.dot(onehot_to(pos_b[...], base, size), rows_b[...], preferred_element_type=jnp.float32)
    out[...] = total.astype(out.dtype)


def pack(h, pos, first, tiles, size):
    width = h.shape[1]
    return pl.pallas_call(
        functools.partial(pack_kernel, first),
        grid=(tiles,),
        in_specs=[
            pl.BlockSpec((1, size), lambda i: (0, i + first)),
            pl.BlockSpec((1, size), lambda i: (0, i + first + 1)),
            pl.BlockSpec((size, width), lambda i: (i + first, 0)),
            pl.BlockSpec((size, width), lambda i: (i + first + 1, 0)),
        ],
        out_specs=pl.BlockSpec((size, width), lambda i: (i, 0)),
        out_shape=jax.ShapeDtypeStruct((tiles * size, width), h.dtype),
        compiler_params=pltpu.CompilerParams(vmem_limit_bytes=VMEM_LIMIT),
        cost_estimate=pl.CostEstimate(
            flops=4 * tiles * size * size * width, bytes_accessed=4 * tiles * size * width, transcendentals=0
        ),
        name="pack_rows",
    )(pos, pos, h, h)


def pack_last_kernel(base, pos, rows, out, total):
    step = pl.program_id(0)
    part = jnp.dot(onehot_to(pos[...], base, out.shape[0]), rows[...], preferred_element_type=jnp.float32)

    @pl.when(step == 0)
    def _():
        total[...] = part

    @pl.when(step > 0)
    def _():
        total[...] += part

    @pl.when(step == pl.num_programs(0) - 1)
    def _():
        out[...] = total[...].astype(out.dtype)


def pack_last(h, pos, base, size):
    rows, width = h.shape
    step = 2 * size
    return pl.pallas_call(
        functools.partial(pack_last_kernel, base),
        grid=(rows // step,),
        in_specs=[
            pl.BlockSpec((1, step), lambda i: (0, i)),
            pl.BlockSpec((step, width), lambda i: (i, 0)),
        ],
        out_specs=pl.BlockSpec((size, width), lambda i: (0, 0)),
        out_shape=jax.ShapeDtypeStruct((size, width), h.dtype),
        scratch_shapes=[pltpu.VMEM((size, width), jnp.float32)],
        compiler_params=pltpu.CompilerParams(vmem_limit_bytes=VMEM_LIMIT),
        cost_estimate=pl.CostEstimate(
            flops=2 * size * rows * width, bytes_accessed=2 * rows * width, transcendentals=0
        ),
        name="pack_last",
    )(pos, h)


def unpack_kernel(first, start, end, has_prev, *refs):
    if has_prev:
        pos, before, here_a, here_b, last, _, out = refs
    else:
        pos, here_a, here_b, last, out = refs
    size = out.shape[0]
    tile = pl.program_id(0) + first
    sources = [
        (here_a, jnp.where(tile - 1 >= start, tile - 1, NOWHERE)),
        (here_b, jnp.where(tile < end, tile, NOWHERE)),
        (last, 7),
    ]
    if has_prev:
        sources.append((before, jnp.where(tile - 1 < start, start - 1, NOWHERE)))
    total = None
    for ref, place in sources:
        onehot = onehot_to(pos[...], place * size, size)
        part = lax.dot_general(
            onehot, ref[...], (((0,), (0,)), ((), ())), preferred_element_type=jnp.float32
        )
        total = part if total is None else total + part
    out[...] = total.astype(out.dtype)


def unpack(pos, before, here, last, out, first, tiles, start, rows, size):
    width = here.shape[1]
    count = here.shape[0] // size
    end = start + count
    specs = [pl.BlockSpec((1, size), lambda i: (0, i + first))]
    args = [pos]
    if before is not None:
        specs.append(pl.BlockSpec((size, width), lambda i: (before.shape[0] // size - 1, 0)))
        args.append(before)
    specs += [
        pl.BlockSpec((size, width), lambda i: (jnp.clip(i + first - 1 - start, 0, count - 1), 0)),
        pl.BlockSpec((size, width), lambda i: (jnp.clip(i + first - start, 0, count - 1), 0)),
        pl.BlockSpec((size, width), lambda i: (0, 0)),
    ]
    args += [here, here, last]
    aliases = {}
    if out is not None:
        aliases = {len(args): 0}
        specs.append(pl.BlockSpec(memory_space=pl.ANY))
        args.append(out)
    return pl.pallas_call(
        functools.partial(unpack_kernel, first, start, end, before is not None),
        grid=(tiles,),
        in_specs=specs,
        out_specs=pl.BlockSpec((size, width), lambda i: (i + first, 0)),
        out_shape=jax.ShapeDtypeStruct((rows, width), here.dtype),
        input_output_aliases=aliases,
        compiler_params=pltpu.CompilerParams(vmem_limit_bytes=VMEM_LIMIT),
        cost_estimate=pl.CostEstimate(
            flops=6 * tiles * size * size * width, bytes_accessed=6 * tiles * size * width, transcendentals=0
        ),
        name="unpack_rows",
    )(*args)


def expert_part(piece, gate_dev, up_dev, down_dev):
    gate = jnp.dot(piece, gate_dev, preferred_element_type=jnp.float32)
    upper = jnp.dot(piece, up_dev, preferred_element_type=jnp.float32)
    active = (jax.nn.silu(gate) * upper).astype(jnp.bfloat16)
    partial_out = jnp.dot(active, down_dev, preferred_element_type=jnp.float32)
    return lax.optimization_barrier(partial_out.astype(jnp.bfloat16))


def local(state, norm_gain, router, w_gate, w_up, w_down, route_ids):
    h = state[0]
    rows = h.shape[0]
    size = rows // 8
    raw_rows = rows - size
    ids = route_ids[0, 0]

    chosen = jnp.sum((ids == 0).astype(jnp.int32), axis=-1)
    slot = jnp.cumsum(chosen) - chosen
    kept = (chosen > 0) & (slot < size)
    count = jnp.minimum(jnp.sum(chosen), size)
    other = jnp.arange(rows, dtype=jnp.int32) - jnp.minimum(slot, size)
    pos = jnp.where(kept, raw_rows + slot, jnp.where(other < raw_rows, other, other + count))
    pos = pos.astype(jnp.int32)[None, :]

    packed, arrived = [], []
    start = 0
    for tiles in CHUNKS:
        packed.append(pack(h, pos, start, tiles, size))
        start += tiles
    moved_pos = passed_along(pos, "section", 1)
    arrived.append(passed_along(packed[0], "section", 1))
    arrived.append(passed_along(packed[1], "section", 1))
    packed[2] = after(packed[2], arrived[0])
    arrived.append(passed_along(packed[2], "section", 1))
    last = pack_last(h, after(pos, packed[1]), raw_rows, size)

    last_ids = jnp.dot(
        onehot_to(pos, raw_rows, size), ids.astype(jnp.bfloat16), preferred_element_type=jnp.float32
    )
    last32 = last.astype(jnp.float32)
    var = jnp.mean(last32 * last32, axis=-1, keepdims=True)
    normed = (last32 * lax.rsqrt(var + 1e-06) * norm_gain[0]).astype(jnp.bfloat16)
    scores = jax.nn.sigmoid(jnp.dot(normed, router[0], preferred_element_type=jnp.float32))
    experts = jnp.arange(router.shape[2]).astype(jnp.float32)
    picked = jnp.sum((last_ids[:, :, None] == experts[None, None, :]).astype(jnp.float32), axis=1)
    weight = 2.5 * scores[:, 0] * picked[:, 0] / jnp.sum(scores * picked, axis=-1)

    both = lax.all_gather(after(normed, (arrived[0], packed[3])), "expert", axis=0, tiled=True)
    partials = expert_part(after(both, arrived[1]), w_gate[0], w_up[0], w_down[0])
    summed = lax.psum_scatter(after(partials, arrived[2]), "expert", scatter_dimension=0, tiled=True).astype(jnp.float32)
    is_kept = (jnp.arange(size) < count)[:, None]
    delta = jnp.where(is_kept, summed * weight[:, None], 0.0)
    updated = (last32 + delta).astype(jnp.bfloat16)

    moved_last = passed_along(updated, "section", 1)
    arrived.append(passed_along(after(packed[3], arrived[2]), "section", 1))

    out, before, start = None, None, 0
    for chunk, tiles in zip(arrived, CHUNKS):
        count = tiles + (start + tiles == 7)
        out = unpack(moved_pos, before, chunk, moved_last, out, start, count, start, rows, size)
        before, start = chunk, start + tiles
    return out[None]


def solution(mesh):
    return jax.shard_map(
        local,
        mesh=mesh,
        in_specs=(
            P("section", "expert", None),
            P("section", None),
            P("section", None, None),
            P("section", None, "expert"),
            P("section", None, "expert"),
            P("section", "expert", None),
            P(None, "section", "expert", None),
        ),
        out_specs=P("section", "expert", None),
        check_vma=False,
    )
```

```python
import functools

import jax
import jax.numpy as jnp
from jax import lax
from jax.experimental import pallas as pl
from jax.experimental.pallas import tpu as pltpu
from jax.sharding import PartitionSpec as P

VMEM_LIMIT = 56 * 1024 * 1024
COLUMN_PARTS = 4
NOWHERE = -(1 << 20)
CHUNKS = (1, 5, 1)
LATER_COST = pl.CostEstimate(flops=1024, bytes_accessed=100000000, transcendentals=0)
SMALL_COST = pl.CostEstimate(flops=1024, bytes_accessed=1024, transcendentals=0)


def passed_along(x, axis, by):
    devices = lax.axis_size(axis)
    return lax.ppermute(x, axis, [(i, (i + by) % devices) for i in range(devices)])


def after(x, done):
    return lax.optimization_barrier((x, done))[0]


def onehot_to(pos, base, size):
    places = lax.broadcasted_iota(jnp.int32, (size, pos.shape[1]), 0) + base
    return jnp.where(places == pos, 1.0, 0.0).astype(jnp.bfloat16)


def pack_kernel(first, pos_a, pos_b, rows_a, rows_b, *refs):
    out = refs[-1]
    size = rows_a.shape[0]
    base = (pl.program_id(0) + first) * size
    onehot = onehot_to(jnp.concatenate([pos_a[...], pos_b[...]], axis=1), base, size)
    rows = jnp.concatenate([rows_a[...], rows_b[...]], axis=0)
    out[:size] = jnp.dot(onehot, rows, preferred_element_type=jnp.float32).astype(out.dtype)
    if len(refs) > 1:
        out[size:] = refs[0][...]


def pack(h, pos, first, tiles, size, cost=SMALL_COST, extra=None):
    width = h.shape[1]
    part = width // COLUMN_PARTS
    more = 0 if extra is None else extra.shape[0]
    assert tiles == 1 or not more
    specs = [
        pl.BlockSpec((1, size), lambda i, j: (0, i + first)),
        pl.BlockSpec((1, size), lambda i, j: (0, i + first + 1)),
        pl.BlockSpec((size, part), lambda i, j: (i + first, j)),
        pl.BlockSpec((size, part), lambda i, j: (i + first + 1, j)),
    ]
    args = [pos, pos, h, h]
    if more:
        specs.append(pl.BlockSpec((more, part), lambda i, j: (0, j)))
        args.append(extra)
    return pl.pallas_call(
        functools.partial(pack_kernel, first),
        grid=(tiles, COLUMN_PARTS),
        in_specs=specs,
        out_specs=pl.BlockSpec((size + more, part), lambda i, j: (i, j)),
        out_shape=jax.ShapeDtypeStruct((tiles * size + more, width), h.dtype),
        compiler_params=pltpu.CompilerParams(vmem_limit_bytes=VMEM_LIMIT),
        cost_estimate=cost,
        name="pack_rows",
    )(*args)


def pack_last_kernel(base, pos, rows, out, total):
    step = pl.program_id(0)
    part = jnp.dot(onehot_to(pos[...], base, out.shape[0]), rows[...], preferred_element_type=jnp.float32)

    @pl.when(step == 0)
    def _():
        total[...] = part

    @pl.when(step > 0)
    def _():
        total[...] += part

    @pl.when(step == pl.num_programs(0) - 1)
    def _():
        out[...] = total[...].astype(out.dtype)


def pack_last(h, pos, base, size):
    rows, width = h.shape
    step = 2 * size
    return pl.pallas_call(
        functools.partial(pack_last_kernel, base),
        grid=(rows // step,),
        in_specs=[
            pl.BlockSpec((1, step), lambda i: (0, i)),
            pl.BlockSpec((step, width), lambda i: (i, 0)),
        ],
        out_specs=pl.BlockSpec((size, width), lambda i: (0, 0)),
        out_shape=jax.ShapeDtypeStruct((size, width), h.dtype),
        scratch_shapes=[pltpu.VMEM((size, width), jnp.float32)],
        compiler_params=pltpu.CompilerParams(vmem_limit_bytes=VMEM_LIMIT),
        cost_estimate=SMALL_COST,
        name="pack_last",
    )(pos, h)


def unpack_kernel(first, windows, aliased, *refs):
    pos, last = refs[0], refs[1]
    sources = refs[2 : 2 + len(windows)]
    out, onehot = refs[2 + len(windows) + aliased :]
    size = last.shape[0]
    tile = pl.program_id(0) * 2 + first

    @pl.when(pl.program_id(1) == 0)
    def _():
        parts = [onehot_to(pos[...], 7 * size, size)]
        for offset, start, end in windows:
            place = tile + offset
            inside = (place >= start) & (place < end)
            parts.append(onehot_to(pos[...], jnp.where(inside, place, NOWHERE) * size, size))
        both = jnp.concatenate([part.astype(jnp.float32) for part in parts], axis=0)
        onehot[...] = both.T.astype(jnp.bfloat16)

    rows = jnp.concatenate([last[...]] + [ref[...] for ref in sources], axis=0)
    out[...] = jnp.dot(onehot[...], rows, preferred_element_type=jnp.float32).astype(out.dtype)


def unpack(pos, pieces, last, out, first, pairs, rows):
    size, width = last.shape
    part = width // COLUMN_PARTS
    specs = [
        pl.BlockSpec((1, 2 * size), lambda i, j: (0, i + first // 2)),
        pl.BlockSpec((size, part), lambda i, j: (0, j)),
    ]
    args = [pos, last]
    windows = []
    for piece, start in pieces:
        count = piece.shape[0] // size
        for offset in (-1, 0, 1):
            places = [first + 2 * pair + offset - start for pair in range(pairs)]
            if any(0 <= place < count for place in places):
                windows.append((offset, start, start + count))
                specs.append(
                    pl.BlockSpec(
                        (size, part),
                        lambda i, j, shift=first + offset - start, count=count: (
                            jnp.clip(2 * i + shift, 0, count - 1),
                            j,
                        ),
                    )
                )
                args.append(piece)
    aliases = {}
    if out is not None:
        aliases = {len(args): 0}
        specs.append(pl.BlockSpec(memory_space=pl.ANY))
        args.append(out)
    depth = size * (len(windows) + 1)
    return pl.pallas_call(
        functools.partial(unpack_kernel, first, tuple(windows), out is not None),
        grid=(pairs, COLUMN_PARTS),
        in_specs=specs,
        out_specs=pl.BlockSpec((2 * size, part), lambda i, j: (i + first // 2, j)),
        out_shape=jax.ShapeDtypeStruct((rows, width), last.dtype),
        scratch_shapes=[pltpu.VMEM((2 * size, depth), jnp.bfloat16)],
        input_output_aliases=aliases,
        compiler_params=pltpu.CompilerParams(vmem_limit_bytes=VMEM_LIMIT),
        cost_estimate=SMALL_COST,
        name="unpack_rows",
    )(*args)


def expert_rows(rows, gate_dev, up_dev, down_dev, out):
    gate = jnp.dot(rows[...], gate_dev[0], preferred_element_type=jnp.float32)
    upper = jnp.dot(rows[...], up_dev[0], preferred_element_type=jnp.float32)
    active = (jax.nn.silu(gate) * upper).astype(jnp.bfloat16)
    part = out.shape[1] // COLUMN_PARTS
    for j in range(COLUMN_PARTS):
        columns = slice(j * part, (j + 1) * part)
        out[:, columns] = jnp.dot(
            active, down_dev[0, :, columns], preferred_element_type=jnp.float32
        ).astype(out.dtype)


def update_kernel(
    last, picked, keep, gain, router, gate_dev, up_dev, down_dev, out,
    normed, normed_got, own_part, sent_part, got_part, sems,
):
    other = 1 - lax.axis_index("expert")
    barrier = pltpu.get_barrier_semaphore()
    pl.semaphore_signal(barrier, inc=1, device_id={"expert": other}, device_id_type=pl.DeviceIdType.MESH)

    last32 = last[...].astype(jnp.float32)
    var = jnp.mean(last32 * last32, axis=-1, keepdims=True)
    normed[...] = (last32 * lax.rsqrt(var + 1e-06) * gain[...]).astype(normed.dtype)
    pl.semaphore_wait(barrier, 1)
    rows_copy = pltpu.make_async_remote_copy(
        src_ref=normed, dst_ref=normed_got, send_sem=sems.at[0], recv_sem=sems.at[1],
        device_id={"expert": other}, device_id_type=pl.DeviceIdType.MESH,
    )
    rows_copy.start()

    scores = jax.nn.sigmoid(jnp.dot(normed[...], router[0], preferred_element_type=jnp.float32))
    named = scores * picked[...]
    weight = 2.5 * named[:, 0:1] / jnp.sum(named, axis=-1, keepdims=True)
    expert_rows(normed, gate_dev, up_dev, down_dev, own_part)

    rows_copy.wait()
    expert_rows(normed_got, gate_dev, up_dev, down_dev, sent_part)
    part_copy = pltpu.make_async_remote_copy(
        src_ref=sent_part, dst_ref=got_part, send_sem=sems.at[2], recv_sem=sems.at[3],
        device_id={"expert": other}, device_id_type=pl.DeviceIdType.MESH,
    )
    part_copy.start()
    part_copy.wait()
    summed = own_part[...].astype(jnp.float32) + got_part[...].astype(jnp.float32)
    delta = jnp.where(keep[...] > 0.0, summed * weight, 0.0)
    out[...] = (last[...].astype(jnp.float32) + delta).astype(out.dtype)


def update(last, picked, keep, norm_gain, router, w_gate, w_up, w_down):
    block = pltpu.VMEM(last.shape, last.dtype)
    return pl.pallas_call(
        update_kernel,
        in_specs=[pl.BlockSpec(memory_space=pltpu.VMEM)] * 8,
        out_specs=pl.BlockSpec(memory_space=pltpu.VMEM),
        out_shape=jax.ShapeDtypeStruct(last.shape, last.dtype),
        scratch_shapes=[block] * 5 + [pltpu.SemaphoreType.DMA((4,))],
        compiler_params=pltpu.CompilerParams(
            collective_id=0, has_side_effects=True, vmem_limit_bytes=VMEM_LIMIT
        ),
        cost_estimate=SMALL_COST,
        name="expert_update",
    )(last, picked, keep, norm_gain, router, w_gate, w_up, w_down)


def local(state, norm_gain, router, w_gate, w_up, w_down, route_ids):
    h = state[0]
    rows = h.shape[0]
    size = rows // 8
    raw_rows = rows - size
    ids = route_ids[0, 0]

    chosen = jnp.sum((ids == 0).astype(jnp.int32), axis=-1)
    slot = jnp.cumsum(chosen) - chosen
    kept = (chosen > 0) & (slot < size)
    count = jnp.minimum(jnp.sum(chosen), size)
    other = jnp.arange(rows, dtype=jnp.int32) - jnp.minimum(slot, size)
    pos = jnp.where(kept, raw_rows + slot, jnp.where(other < raw_rows, other, other + count))
    pos = pos.astype(jnp.int32)[None, :]

    places = jnp.concatenate([pos // 256, pos % 256], axis=1).astype(h.dtype)
    extra = jnp.pad(places, ((0, 15), (0, h.shape[1] - 2 * rows)))
    packed = [pack(h, pos, 0, CHUNKS[0], size, extra=extra)]
    packed.append(pack(h, after(pos, packed), CHUNKS[0], CHUNKS[1], size))
    moved = [passed_along(packed[0], "section", 1), passed_along(packed[1], "section", 1)]
    start = CHUNKS[0] + CHUNKS[1]
    packed.append(pack(h, after(pos, moved[0]), start, CHUNKS[2], size, LATER_COST))
    moved.append(passed_along(after(packed[2], moved[1]), "section", 1))
    places = moved[0][size].astype(jnp.int32)
    moved_pos = (places[:rows] * 256 + places[rows : 2 * rows])[None, :]
    last = pack_last(h, after(pos, packed[:2]), raw_rows, size)

    last_ids = jnp.dot(
        onehot_to(pos, raw_rows, size), ids.astype(jnp.bfloat16), preferred_element_type=jnp.float32
    )
    experts = jnp.arange(router.shape[2]).astype(jnp.float32)
    picked = jnp.sum((last_ids[:, :, None] == experts[None, None, :]).astype(jnp.float32), axis=1)
    keep = (jnp.arange(size) < count).astype(jnp.float32)[:, None]
    updated = update(last, picked, keep, norm_gain, router, w_gate, w_up, w_down)
    moved_last = passed_along(updated, "section", 1)

    pieces = [(moved[0], 0), (moved[1], 1), (moved[2], 6)]
    out = unpack(moved_pos, pieces[:2], moved_last, None, 0, 3, rows)
    out = unpack(moved_pos, pieces[1:], moved_last, out, 6, 1, rows)
    return out[None]


def solution(mesh):
    return jax.shard_map(
        local,
        mesh=mesh,
        in_specs=(
            P("section", "expert", None),
            P("section", None),
            P("section", None, None),
            P("section", None, "expert"),
            P("section", None, "expert"),
            P("section", "expert", None),
            P(None, "section", "expert", None),
        ),
        out_specs=P("section", "expert", None),
        check_vma=False,
    )
```

```python
import functools

import jax
import jax.numpy as jnp
from jax import lax
from jax.experimental import pallas as pl
from jax.experimental.pallas import tpu as pltpu
from jax.sharding import PartitionSpec as P

VMEM_LIMIT = 56 * 1024 * 1024
COLUMN_PARTS = 4
EARLY = 3
SMALL_COST = pl.CostEstimate(flops=1024, bytes_accessed=1024, transcendentals=0)
PARAMS = pltpu.CompilerParams(vmem_limit_bytes=VMEM_LIMIT)


def passed_along(x, axis, by):
    devices = lax.axis_size(axis)
    return lax.ppermute(x, axis, [(i, (i + by) % devices) for i in range(devices)])


def after(x, done):
    return lax.optimization_barrier((x, done))[0]


def onehot_to(pos, base, size):
    places = lax.broadcasted_iota(jnp.int32, (size, pos.shape[1]), 0) + base
    return jnp.where(places == pos, 1.0, 0.0).astype(jnp.bfloat16)


def pack_kernel(base, with_places, pos, rows, out):
    size = out.shape[0] - (16 if with_places else 0)
    count = rows.shape[0]
    onehot = onehot_to(pos[...], base, size)
    out[:size] = jnp.dot(onehot, rows[...], preferred_element_type=jnp.float32).astype(out.dtype)
    if with_places:
        out[size:] = jnp.zeros((16, out.shape[1]), out.dtype)

        @pl.when(pl.program_id(0) == 0)
        def _():
            lines = jnp.concatenate(
                [pos[:, i * 128 : (i + 1) * 128] for i in range(count // 128)] + [jnp.zeros((8 - count // 128, 128), jnp.int32)],
                axis=0,
            )
            both = jnp.concatenate([lines // 256, lines % 256], axis=0)
            out[size:, :128] = both.astype(jnp.float32).astype(out.dtype)


def pack(h, pos, base, size, with_places):
    width = h.shape[1]
    part = width // COLUMN_PARTS
    count = pos.shape[1]
    out_rows = size + (16 if with_places else 0)
    return pl.pallas_call(
        functools.partial(pack_kernel, base, with_places),
        grid=(COLUMN_PARTS,),
        in_specs=[pl.BlockSpec((1, count), lambda j: (0, 0)), pl.BlockSpec((count, part), lambda j: (0, j))],
        out_specs=pl.BlockSpec((out_rows, part), lambda j: (0, j)),
        out_shape=jax.ShapeDtypeStruct((out_rows, width), h.dtype),
        compiler_params=PARAMS,
        cost_estimate=SMALL_COST,
        name="pack_rows",
    )(pos, h)


def merge_kernel(slots, rows, changed, out, onehot):
    size = rows.shape[0]

    @pl.when(pl.program_id(1) == 0)
    def _():
        line = lax.broadcasted_iota(jnp.int32, (size, size), 0)
        lane = lax.broadcasted_iota(jnp.int32, (size, size), 1)
        own = jnp.where((line == lane) & (slots[...] < 0), 1.0, 0.0)
        other = jnp.where(line == slots[...], 1.0, 0.0)
        onehot[...] = jnp.concatenate([own, other], axis=0).T.astype(jnp.bfloat16)

    both = jnp.concatenate([rows[...], changed[...]], axis=0)
    out[...] = jnp.dot(onehot[...], both, preferred_element_type=jnp.float32).astype(out.dtype)


def merge(h, slots, changed, first, tiles):
    size, width = changed.shape
    part = width // COLUMN_PARTS
    return pl.pallas_call(
        merge_kernel,
        grid=(tiles, COLUMN_PARTS),
        in_specs=[
            pl.BlockSpec((1, size), lambda i, j: (0, i + first)),
            pl.BlockSpec((size, part), lambda i, j: (i + first, j)),
            pl.BlockSpec((size, part), lambda i, j: (0, j)),
        ],
        out_specs=pl.BlockSpec((size, part), lambda i, j: (i, j)),
        out_shape=jax.ShapeDtypeStruct((tiles * size, width), h.dtype),
        scratch_shapes=[pltpu.VMEM((size, 2 * size), jnp.bfloat16)],
        compiler_params=PARAMS,
        cost_estimate=SMALL_COST,
        name="merge_rows",
    )(slots, h, changed)


def unpack_kernel(pos, early, late, out, onehot):
    @pl.when(pl.program_id(0) == 0)
    def _():
        onehot[...] = onehot_to(pos[...], 0, pos.shape[1]).astype(jnp.float32).T.astype(jnp.bfloat16)

    both = jnp.concatenate([early[...], late[...]], axis=0)
    out[...] = jnp.dot(onehot[...], both, preferred_element_type=jnp.float32).astype(out.dtype)


def unpack(pos, early, late, rows):
    size, width = late.shape
    part = width // COLUMN_PARTS
    count = pos.shape[1]
    return pl.pallas_call(
        unpack_kernel,
        grid=(COLUMN_PARTS,),
        in_specs=[
            pl.BlockSpec((1, count), lambda j: (0, 0)),
            pl.BlockSpec((count - size, part), lambda j: (0, j)),
            pl.BlockSpec((size, part), lambda j: (0, j)),
        ],
        out_specs=pl.BlockSpec((count, part), lambda j: (0, j)),
        out_shape=jax.ShapeDtypeStruct((rows, width), late.dtype),
        scratch_shapes=[pltpu.VMEM((count, count), jnp.bfloat16)],
        compiler_params=PARAMS,
        cost_estimate=SMALL_COST,
        name="unpack_rows",
    )(pos, early, late)


def put_kernel(piece, _, out):
    out[...] = piece[...]


def put(out, piece, first_row):
    step = 64
    width = piece.shape[1]
    return pl.pallas_call(
        put_kernel,
        grid=(piece.shape[0] // step,),
        in_specs=[pl.BlockSpec((step, width), lambda i: (i, 0)), pl.BlockSpec(memory_space=pl.ANY)],
        out_specs=pl.BlockSpec((step, width), lambda i: (i + first_row // step, 0)),
        out_shape=jax.ShapeDtypeStruct(out.shape, out.dtype),
        input_output_aliases={1: 0},
        compiler_params=PARAMS,
        cost_estimate=SMALL_COST,
        name="put_rows",
    )(piece, out)


def pack_last_kernel(base, pos, rows, out, total):
    step = pl.program_id(0)
    part = jnp.dot(onehot_to(pos[...], base, out.shape[0]), rows[...], preferred_element_type=jnp.float32)

    @pl.when(step == 0)
    def _():
        total[...] = part

    @pl.when(step > 0)
    def _():
        total[...] += part

    @pl.when(step == pl.num_programs(0) - 1)
    def _():
        out[...] = total[...].astype(out.dtype)


def pack_last(h, pos, base, size):
    rows, width = h.shape
    step = 2 * size
    return pl.pallas_call(
        functools.partial(pack_last_kernel, base),
        grid=(rows // step,),
        in_specs=[
            pl.BlockSpec((1, step), lambda i: (0, i)),
            pl.BlockSpec((step, width), lambda i: (i, 0)),
        ],
        out_specs=pl.BlockSpec((size, width), lambda i: (0, 0)),
        out_shape=jax.ShapeDtypeStruct((size, width), h.dtype),
        scratch_shapes=[pltpu.VMEM((size, width), jnp.float32)],
        compiler_params=pltpu.CompilerParams(vmem_limit_bytes=VMEM_LIMIT),
        cost_estimate=SMALL_COST,
        name="pack_last",
    )(pos, h)


def expert_rows(rows, gate_dev, up_dev, down_dev, out):
    gate = jnp.dot(rows[...], gate_dev[0], preferred_element_type=jnp.float32)
    upper = jnp.dot(rows[...], up_dev[0], preferred_element_type=jnp.float32)
    active = (jax.nn.silu(gate) * upper).astype(jnp.bfloat16)
    part = out.shape[1] // COLUMN_PARTS
    for j in range(COLUMN_PARTS):
        columns = slice(j * part, (j + 1) * part)
        out[:, columns] = jnp.dot(
            active, down_dev[0, :, columns], preferred_element_type=jnp.float32
        ).astype(out.dtype)


def update_kernel(
    last, picked, beside, keep, gain, router, gate_dev, up_dev, down_dev, out, out_beside,
    normed, normed_got, own_part, sent_part, got_part, sems,
):
    other = 1 - lax.axis_index("expert")
    barrier = pltpu.get_barrier_semaphore()
    pl.semaphore_signal(barrier, inc=1, device_id={"expert": other}, device_id_type=pl.DeviceIdType.MESH)

    last32 = last[...].astype(jnp.float32)
    var = jnp.mean(last32 * last32, axis=-1, keepdims=True)
    normed[...] = (last32 * lax.rsqrt(var + 1e-06) * gain[...]).astype(normed.dtype)
    pl.semaphore_wait(barrier, 1)
    rows_copy = pltpu.make_async_remote_copy(
        src_ref=normed, dst_ref=normed_got, send_sem=sems.at[0], recv_sem=sems.at[1],
        device_id={"expert": other}, device_id_type=pl.DeviceIdType.MESH,
    )
    rows_copy.start()

    scores = jax.nn.sigmoid(jnp.dot(normed[...], router[0], preferred_element_type=jnp.float32))
    named = scores * picked[...]
    weight = 2.5 * named[:, 0:1] / jnp.sum(named, axis=-1, keepdims=True)
    expert_rows(normed, gate_dev, up_dev, down_dev, own_part)

    rows_copy.wait()
    expert_rows(normed_got, gate_dev, up_dev, down_dev, sent_part)
    part_copy = pltpu.make_async_remote_copy(
        src_ref=sent_part, dst_ref=got_part, send_sem=sems.at[2], recv_sem=sems.at[3],
        device_id={"expert": other}, device_id_type=pl.DeviceIdType.MESH,
    )
    part_copy.start()
    part_copy.wait()
    summed = own_part[...].astype(jnp.float32) + got_part[...].astype(jnp.float32)
    out[...] = (last[...].astype(jnp.float32) + summed * weight).astype(out.dtype)
    out_beside[...] = jnp.where(keep[...] > 0.0, out[...].astype(jnp.float32), beside[...].astype(jnp.float32)).astype(out.dtype)


def update(last, picked, beside, keep, norm_gain, router, w_gate, w_up, w_down):
    block = pltpu.VMEM(last.shape, last.dtype)
    return pl.pallas_call(
        update_kernel,
        in_specs=[pl.BlockSpec(memory_space=pltpu.VMEM)] * 9,
        out_specs=[pl.BlockSpec(memory_space=pltpu.VMEM)] * 2,
        out_shape=[jax.ShapeDtypeStruct(last.shape, last.dtype)] * 2,
        scratch_shapes=[block] * 5 + [pltpu.SemaphoreType.DMA((4,))],
        compiler_params=pltpu.CompilerParams(
            collective_id=0, has_side_effects=True, vmem_limit_bytes=VMEM_LIMIT
        ),
        cost_estimate=SMALL_COST,
        name="expert_update",
    )(last, picked, beside, keep, norm_gain, router, w_gate, w_up, w_down)


def local(state, norm_gain, router, w_gate, w_up, w_down, route_ids):
    h = state[0]
    rows = h.shape[0]
    size = rows // 8
    early_rows = EARLY * size
    head_rows = early_rows + size
    ids = route_ids[0, 0]

    chosen = jnp.sum((ids == 0).astype(jnp.int32), axis=-1)
    slot = (jnp.cumsum(chosen) - chosen).astype(jnp.int32)
    kept = (chosen > 0) & (slot < size)
    slots = jnp.where(kept, slot, -1)[None, :]
    count = jnp.minimum(jnp.sum(chosen[:head_rows]), size)
    other = jnp.arange(rows, dtype=jnp.int32) - jnp.minimum(slot, size)
    pos = jnp.where(kept, early_rows + slot, jnp.where(other < early_rows, other, other + count))
    pos = pos[None, :head_rows].astype(jnp.int32)

    early = pack(h, pos, 0, early_rows, True)
    moved_early = passed_along(early, "section", 1)
    slots = after(slots, early)
    last = pack_last(h, slots, 0, size)
    beside = pack(h, after(pos, early), early_rows, size, False)

    last_ids = jnp.dot(
        onehot_to(slots, 0, size), ids.astype(jnp.bfloat16), preferred_element_type=jnp.float32
    )
    experts = jnp.arange(router.shape[2]).astype(jnp.float32)
    picked = jnp.sum((last_ids[:, :, None] == experts[None, None, :]).astype(jnp.float32), axis=1)
    keep = (jnp.arange(size) < count).astype(jnp.float32)[:, None]
    changed, beside = update(last, picked, beside, keep, norm_gain, router, w_gate, w_up, w_down)
    moved_beside = passed_along(beside, "section", 1)

    first = EARLY + 1
    second = merge(h, slots, changed, first, 2)
    third = merge(h, slots, after(changed, second), first + 2, 1)
    fourth = merge(h, slots, after(changed, third), first + 3, 1)
    moved_second = passed_along(second, "section", 1)
    moved_third = passed_along(after(third, moved_early), "section", 1)
    moved_fourth = passed_along(after(fourth, moved_second), "section", 1)

    places = moved_early[early_rows:, :128].astype(jnp.int32)
    lines = head_rows // 128
    moved_pos = (places[:lines] * 256 + places[8 : 8 + lines]).reshape(1, head_rows)
    out = unpack(moved_pos, moved_early, moved_beside, rows)
    out = put(out, moved_second, first * size)
    out = put(out, moved_third, (first + 2) * size)
    out = put(out, moved_fourth, (first + 3) * size)
    return out[None]


def solution(mesh):
    return jax.shard_map(
        local,
        mesh=mesh,
        in_specs=(
            P("section", "expert", None),
            P("section", None),
            P("section", None, None),
            P("section", None, "expert"),
            P("section", None, "expert"),
            P("section", "expert", None),
            P(None, "section", "expert", None),
        ),
        out_specs=P("section", "expert", None),
        check_vma=False,
    )
```

```python
import functools

import jax
import jax.numpy as jnp
from jax import lax
from jax.experimental import pallas as pl
from jax.experimental.pallas import tpu as pltpu
from jax.sharding import PartitionSpec as P

VMEM_LIMIT = 56 * 1024 * 1024
COLUMN_PARTS = 4
EARLY = 2
SMALL_COST = pl.CostEstimate(flops=1024, bytes_accessed=1024, transcendentals=0)
PARAMS = pltpu.CompilerParams(vmem_limit_bytes=VMEM_LIMIT)


def passed_along(x, axis, by):
    devices = lax.axis_size(axis)
    return lax.ppermute(x, axis, [(i, (i + by) % devices) for i in range(devices)])


def after(x, done):
    return lax.optimization_barrier((x, done))[0]


def onehot_to(pos, base, size):
    places = lax.broadcasted_iota(jnp.int32, (size, pos.shape[1]), 0) + base
    return jnp.where(places == pos, 1.0, 0.0).astype(jnp.bfloat16)


def pack_early_kernel(cap, chosen, rows, out, pos):
    size = out.shape[0] - 16
    count = rows.shape[0]

    @pl.when(pl.program_id(0) == 0)
    def _():
        line = lax.broadcasted_iota(jnp.int32, (count, count), 0)
        lane = lax.broadcasted_iota(jnp.int32, (count, count), 1)
        ahead = jnp.where(line < lane, 1.0, 0.0).astype(jnp.bfloat16)
        named = chosen[...]
        flags = jnp.broadcast_to(named, (16, count)).astype(jnp.bfloat16)
        slot = jnp.dot(flags, ahead, preferred_element_type=jnp.float32)[0:1].astype(jnp.int32)
        total = jnp.minimum(jnp.sum(named, axis=1, keepdims=True).astype(jnp.int32), cap)
        other = lane[0:1] - jnp.minimum(slot, cap)
        late = jnp.where(other < size, other, other + total)
        places = jnp.where((named > 0.0) & (slot < cap), size + slot, late)
        pos[...] = places
        lines = jnp.concatenate(
            [places[:, i * 128 : (i + 1) * 128] for i in range(count // 128)]
            + [jnp.zeros((8 - count // 128, 128), jnp.int32)],
            axis=0,
        )
        both = jnp.concatenate([lines // 256, lines % 256], axis=0)
        out[size:, :128] = both.astype(jnp.float32).astype(out.dtype)
        out[size:, 128:] = jnp.zeros((16, out.shape[1] - 128), out.dtype)

    @pl.when(pl.program_id(0) > 0)
    def _():
        out[size:] = jnp.zeros((16, out.shape[1]), out.dtype)

    onehot = onehot_to(pos[...], 0, size)
    out[:size] = jnp.dot(onehot, rows[...], preferred_element_type=jnp.float32).astype(out.dtype)


def pack_early(h, chosen, size, cap):
    width = h.shape[1]
    part = width // COLUMN_PARTS
    count = size + cap
    return pl.pallas_call(
        functools.partial(pack_early_kernel, cap),
        grid=(COLUMN_PARTS,),
        in_specs=[pl.BlockSpec((1, count), lambda j: (0, 0)), pl.BlockSpec((count, part), lambda j: (0, j))],
        out_specs=pl.BlockSpec((size + 16, part), lambda j: (0, j)),
        out_shape=jax.ShapeDtypeStruct((size + 16, width), h.dtype),
        scratch_shapes=[pltpu.VMEM((1, count), jnp.int32)],
        compiler_params=PARAMS,
        cost_estimate=SMALL_COST,
        name="pack_early",
    )(chosen, h)


def pack_kernel(base, pos, rows, out):
    onehot = onehot_to(pos[...], base, out.shape[0])
    out[...] = jnp.dot(onehot, rows[...], preferred_element_type=jnp.float32).astype(out.dtype)


def pack(h, pos, base, size):
    width = h.shape[1]
    part = width // COLUMN_PARTS
    count = pos.shape[1]
    return pl.pallas_call(
        functools.partial(pack_kernel, base),
        grid=(COLUMN_PARTS,),
        in_specs=[pl.BlockSpec((1, count), lambda j: (0, 0)), pl.BlockSpec((count, part), lambda j: (0, j))],
        out_specs=pl.BlockSpec((size, part), lambda j: (0, j)),
        out_shape=jax.ShapeDtypeStruct((size, width), h.dtype),
        compiler_params=PARAMS,
        cost_estimate=SMALL_COST,
        name="pack_rows",
    )(pos, h)


def merge_kernel(slots, rows, changed, out, onehot):
    size = rows.shape[0]

    @pl.when(pl.program_id(1) == 0)
    def _():
        line = lax.broadcasted_iota(jnp.int32, (size, size), 0)
        lane = lax.broadcasted_iota(jnp.int32, (size, size), 1)
        own = jnp.where((line == lane) & (slots[...] < 0), 1.0, 0.0)
        other = jnp.where(line == slots[...], 1.0, 0.0)
        onehot[...] = jnp.concatenate([own, other], axis=0).T.astype(jnp.bfloat16)

    both = jnp.concatenate([rows[...], changed[...]], axis=0)
    out[...] = jnp.dot(onehot[...], both, preferred_element_type=jnp.float32).astype(out.dtype)


def merge(h, slots, changed, first, tiles):
    size, width = changed.shape
    part = width // COLUMN_PARTS
    return pl.pallas_call(
        merge_kernel,
        grid=(tiles, COLUMN_PARTS),
        in_specs=[
            pl.BlockSpec((1, size), lambda i, j: (0, i + first)),
            pl.BlockSpec((size, part), lambda i, j: (i + first, j)),
            pl.BlockSpec((size, part), lambda i, j: (0, j)),
        ],
        out_specs=pl.BlockSpec((size, part), lambda i, j: (i, j)),
        out_shape=jax.ShapeDtypeStruct((tiles * size, width), h.dtype),
        scratch_shapes=[pltpu.VMEM((size, 2 * size), jnp.bfloat16)],
        compiler_params=PARAMS,
        cost_estimate=SMALL_COST,
        name="merge_rows",
    )(slots, h, changed)


def unpack_kernel(pos, early, late, out, onehot):
    @pl.when(pl.program_id(0) == 0)
    def _():
        onehot[...] = onehot_to(pos[...], 0, pos.shape[1]).astype(jnp.float32).T.astype(jnp.bfloat16)

    both = jnp.concatenate([early[...], late[...]], axis=0)
    out[...] = jnp.dot(onehot[...], both, preferred_element_type=jnp.float32).astype(out.dtype)


def unpack(pos, early, late, rows):
    size, width = late.shape
    part = width // COLUMN_PARTS
    count = pos.shape[1]
    return pl.pallas_call(
        unpack_kernel,
        grid=(COLUMN_PARTS,),
        in_specs=[
            pl.BlockSpec((1, count), lambda j: (0, 0)),
            pl.BlockSpec((count - size, part), lambda j: (0, j)),
            pl.BlockSpec((size, part), lambda j: (0, j)),
        ],
        out_specs=pl.BlockSpec((count, part), lambda j: (0, j)),
        out_shape=jax.ShapeDtypeStruct((rows, width), late.dtype),
        scratch_shapes=[pltpu.VMEM((count, count), jnp.bfloat16)],
        compiler_params=PARAMS,
        cost_estimate=SMALL_COST,
        name="unpack_rows",
    )(pos, early, late)


def put_kernel(first_row, piece, _, out, sem):
    copy = pltpu.make_async_copy(piece, out.at[pl.ds(first_row, piece.shape[0])], sem)
    copy.start()
    copy.wait()


def put(out, piece, first_row):
    return pl.pallas_call(
        functools.partial(put_kernel, first_row),
        in_specs=[pl.BlockSpec(memory_space=pl.ANY)] * 2,
        out_specs=pl.BlockSpec(memory_space=pl.ANY),
        out_shape=jax.ShapeDtypeStruct(out.shape, out.dtype),
        scratch_shapes=[pltpu.SemaphoreType.DMA],
        input_output_aliases={1: 0},
        compiler_params=pltpu.CompilerParams(vmem_limit_bytes=1024 * 1024),
        cost_estimate=SMALL_COST,
        name="put_rows",
    )(piece, out)


def pack_last_kernel(base, pos, rows, out, total):
    step = pl.program_id(0)
    part = jnp.dot(onehot_to(pos[...], base, out.shape[0]), rows[...], preferred_element_type=jnp.float32)

    @pl.when(step == 0)
    def _():
        total[...] = part

    @pl.when(step > 0)
    def _():
        total[...] += part

    @pl.when(step == pl.num_programs(0) - 1)
    def _():
        out[...] = total[...].astype(out.dtype)


def pack_last(h, pos, base, size):
    rows, width = h.shape
    step = 2 * size
    return pl.pallas_call(
        functools.partial(pack_last_kernel, base),
        grid=(rows // step,),
        in_specs=[
            pl.BlockSpec((1, step), lambda i: (0, i)),
            pl.BlockSpec((step, width), lambda i: (i, 0)),
        ],
        out_specs=pl.BlockSpec((size, width), lambda i: (0, 0)),
        out_shape=jax.ShapeDtypeStruct((size, width), h.dtype),
        scratch_shapes=[pltpu.VMEM((size, width), jnp.float32)],
        compiler_params=pltpu.CompilerParams(vmem_limit_bytes=VMEM_LIMIT),
        cost_estimate=SMALL_COST,
        name="pack_last",
    )(pos, h)


def expert_rows(rows, gate_dev, up_dev, down_dev, out):
    gate = jnp.dot(rows[...], gate_dev[0], preferred_element_type=jnp.float32)
    upper = jnp.dot(rows[...], up_dev[0], preferred_element_type=jnp.float32)
    active = (jax.nn.silu(gate) * upper).astype(jnp.bfloat16)
    part = out.shape[1] // COLUMN_PARTS
    for j in range(COLUMN_PARTS):
        columns = slice(j * part, (j + 1) * part)
        out[:, columns] = jnp.dot(
            active, down_dev[0, :, columns], preferred_element_type=jnp.float32
        ).astype(out.dtype)


def update_kernel(
    last, picked, beside, keep, gain, router, gate_dev, up_dev, down_dev, out, out_beside,
    normed, normed_got, own_part, sent_part, got_part, sems,
):
    other = 1 - lax.axis_index("expert")
    barrier = pltpu.get_barrier_semaphore()
    pl.semaphore_signal(barrier, inc=1, device_id={"expert": other}, device_id_type=pl.DeviceIdType.MESH)

    last32 = last[...].astype(jnp.float32)
    var = jnp.mean(last32 * last32, axis=-1, keepdims=True)
    normed[...] = (last32 * lax.rsqrt(var + 1e-06) * gain[...]).astype(normed.dtype)
    pl.semaphore_wait(barrier, 1)
    rows_copy = pltpu.make_async_remote_copy(
        src_ref=normed, dst_ref=normed_got, send_sem=sems.at[0], recv_sem=sems.at[1],
        device_id={"expert": other}, device_id_type=pl.DeviceIdType.MESH,
    )
    rows_copy.start()

    scores = jax.nn.sigmoid(jnp.dot(normed[...], router[0], preferred_element_type=jnp.float32))
    named = scores * picked[...]
    weight = 2.5 * named[:, 0:1] / jnp.sum(named, axis=-1, keepdims=True)
    expert_rows(normed, gate_dev, up_dev, down_dev, own_part)

    rows_copy.wait()
    expert_rows(normed_got, gate_dev, up_dev, down_dev, sent_part)
    part_copy = pltpu.make_async_remote_copy(
        src_ref=sent_part, dst_ref=got_part, send_sem=sems.at[2], recv_sem=sems.at[3],
        device_id={"expert": other}, device_id_type=pl.DeviceIdType.MESH,
    )
    part_copy.start()
    part_copy.wait()
    summed = own_part[...].astype(jnp.float32) + got_part[...].astype(jnp.float32)
    out[...] = (last[...].astype(jnp.float32) + summed * weight).astype(out.dtype)
    out_beside[...] = jnp.where(keep[...] > 0.0, out[...].astype(jnp.float32), beside[...].astype(jnp.float32)).astype(out.dtype)


def update(last, picked, beside, keep, norm_gain, router, w_gate, w_up, w_down):
    block = pltpu.VMEM(last.shape, last.dtype)
    return pl.pallas_call(
        update_kernel,
        in_specs=[pl.BlockSpec(memory_space=pltpu.VMEM)] * 9,
        out_specs=[pl.BlockSpec(memory_space=pltpu.VMEM)] * 2,
        out_shape=[jax.ShapeDtypeStruct(last.shape, last.dtype)] * 2,
        scratch_shapes=[block] * 5 + [pltpu.SemaphoreType.DMA((4,))],
        compiler_params=pltpu.CompilerParams(
            collective_id=0, has_side_effects=True, vmem_limit_bytes=VMEM_LIMIT
        ),
        cost_estimate=SMALL_COST,
        name="expert_update",
    )(last, picked, beside, keep, norm_gain, router, w_gate, w_up, w_down)


def local(state, norm_gain, router, w_gate, w_up, w_down, route_ids):
    h = state[0]
    rows = h.shape[0]
    size = rows // 8
    early_rows = EARLY * size
    head_rows = early_rows + size
    ids = route_ids[0, 0]

    chosen = jnp.sum((ids == 0).astype(jnp.int32), axis=-1)
    slot = (jnp.cumsum(chosen) - chosen).astype(jnp.int32)
    kept = (chosen > 0) & (slot < size)
    slots = jnp.where(kept, slot, -1)[None, :]
    count = jnp.minimum(jnp.sum(chosen[:head_rows]), size)
    other = jnp.arange(rows, dtype=jnp.int32) - jnp.minimum(slot, size)
    pos = jnp.where(kept, early_rows + slot, jnp.where(other < early_rows, other, other + count))
    pos = pos[None, :head_rows].astype(jnp.int32)

    early = pack_early(h, chosen.astype(jnp.float32)[None, :], early_rows, size)
    moved_early = passed_along(early, "section", 1)
    slots = after(slots, early)
    last = pack_last(h, slots, 0, size)
    beside = pack(h, after(pos, early), early_rows, size)

    last_ids = jnp.dot(
        onehot_to(slots, 0, size), ids.astype(jnp.bfloat16), preferred_element_type=jnp.float32
    )
    experts = jnp.arange(router.shape[2]).astype(jnp.float32)
    picked = jnp.sum((last_ids[:, :, None] == experts[None, None, :]).astype(jnp.float32), axis=1)
    keep = (jnp.arange(size) < count).astype(jnp.float32)[:, None]
    changed, beside = update(last, picked, beside, keep, norm_gain, router, w_gate, w_up, w_down)
    moved_beside = passed_along(beside, "section", 1)

    first = EARLY + 1
    second = merge(h, slots, changed, first, 2)
    third = merge(h, slots, after(changed, second), first + 2, 2)
    fourth = merge(h, slots, after(changed, third), first + 4, 1)
    moved_second = passed_along(second, "section", 1)
    moved_third = passed_along(after(third, moved_early), "section", 1)
    moved_fourth = passed_along(after(fourth, moved_second), "section", 1)

    places = moved_early[early_rows:, :128].astype(jnp.int32)
    lines = head_rows // 128
    moved_pos = (places[:lines] * 256 + places[8 : 8 + lines]).reshape(1, head_rows)
    out = unpack(moved_pos, moved_early, moved_beside, rows)
    out = put(out, moved_second, first * size)
    out = put(out, moved_third, (first + 2) * size)
    out = put(out, moved_fourth, (first + 4) * size)
    return out[None]


def solution(mesh):
    return jax.shard_map(
        local,
        mesh=mesh,
        in_specs=(
            P("section", "expert", None),
            P("section", None),
            P("section", None, None),
            P("section", None, "expert"),
            P("section", None, "expert"),
            P("section", "expert", None),
            P(None, "section", "expert", None),
        ),
        out_specs=P("section", "expert", None),
        check_vma=False,
    )
```
